128 devices in a mesh: face: 32 (over y, x, core), sub: 4 (over z).
Axes of the slice: x: 4, y: 4, z: 4, core: 2. Of those that a mesh axis runs over, the one named last changes fastest.
Arguments:
- h_band: bfloat16 [2, 131072, 256], P(None, ('face', 'sub')), may hold values from -6 to 6
- edges_in: bfloat16 [2, 786432, 256], P(None, ('face', 'sub')), may hold values from -6 to 6
- band_pick: int32 [131072], P(('face', 'sub')), may hold values from 0 to 1023, as said below
- senders: int32 [786432], P(('face', 'sub')), may hold values from 0 to 1279, as said below
- receivers: int32 [786432], P(('face', 'sub')), may hold values from 0 to 1023
- halo_rows: int32 [16384], P(('face', 'sub')), may hold values from 0 to 1023, as said below
- w_edge_in: bfloat16 [768, 256], P(('face', 'sub')), may hold values from -0.21875 to 0.21875
- w_edge_out: bfloat16 [256, 256], P(('face', 'sub')), may hold values from -0.375 to 0.375
- w_node_in: bfloat16 [512, 256], P(('face', 'sub')), may hold values from -0.25 to 0.25
- w_node_out: bfloat16 [256, 256], P(('face', 'sub')), may hold values from -0.375 to 0.375
- biases: bfloat16 [256, 4], P(('face', 'sub')), may hold values from -3 to 3
- norm_gain: bfloat16 [256, 2], P(('face', 'sub')), may hold values from 0.099609375 to 1.8984375
- norm_shift: bfloat16 [256, 2], P(('face', 'sub')), may hold values from -3 to 3
- cot_nodes: bfloat16 [2, 131072, 256], P(None, ('face', 'sub')), may hold values from -6 to 6
- cot_edges: bfloat16 [2, 786432, 256], P(None, ('face', 'sub')), may hold values from -6 to 6
Outputs:
- node_out: bfloat16 [2, 131072, 256], P(None, ('face', 'sub'))
- edge_out: bfloat16 [2, 786432, 256], P(None, ('face', 'sub'))
- grad_nodes: bfloat16 [2, 131072, 256], P(None, ('face', 'sub'))
- grad_edges: bfloat16 [2, 786432, 256], P(None, ('face', 'sub'))
- grad_edge_in: float32 [768, 256], P(('face', 'sub'))
- grad_edge_out: float32 [256, 256], P(('face', 'sub'))
- grad_node_in: float32 [512, 256], P(('face', 'sub'))
- grad_node_out: float32 [256, 256], P(('face', 'sub'))
- grad_biases: float32 [256, 4], P(('face', 'sub'))
- grad_gain: float32 [256, 2], P(('face', 'sub'))
- grad_shift: float32 [256, 2], P(('face', 'sub'))
The draws below stay inside these ranges and needn't reach their ends.
Inputs may be any that keep to these rules, and one draw needn't show every extreme that they name: `band_pick`: on each device, a permutation of 0 .. 1023. `senders`: rows of the device's table: below 1024 its own nodes, then 128 rows from the previous face device, then 128 from the next. `halo_rows`: on each device, 128 distinct local rows.
All inputs are finite; a program needn't handle non-finite values.
Results may differ from the reference program's by a relative error of at most 0.0079.
Values may be sent and summed in bfloat16 or wider, within the bound.
A program may use at most 256 MiB of HBM per device.

```python
import jax
import jax.numpy as jnp
from jax import lax

L = 256
NODE_DEV = 1024
MICRO = 2
EDGE_DEV = 6144
HALO = 128
NODES = 131072
EDGES = 786432
N_FACE = 32
N_SUB = 4


def local_orders(key, count):
    keys = jax.random.split(key, NODES // NODE_DEV)
    orders = jax.vmap(lambda single: jax.random.permutation(single, NODE_DEV))(keys)
    return orders[:, :count].reshape(-1).astype(jnp.int32)


def draw_band_pick(key, part):
    key = jax.random.fold_in(key, 11)
    return local_orders(key, NODE_DEV)


def draw_halo_rows(key, part):
    key = jax.random.fold_in(key, 12)
    return local_orders(key, HALO)


def draw_senders(key, part):
    key = jax.random.fold_in(key, 13)
    return jax.random.randint(key, (EDGES,), 0, NODE_DEV + 2 * HALO).astype(jnp.int32)


def draw_receivers(key, part):
    key = jax.random.fold_in(key, 14)
    return jax.random.randint(key, (EDGES,), 0, NODE_DEV).astype(jnp.int32)


def levels(own_key, shape, cuts, smallest, top_value):
    factor_of = 1.0
    for position, shards_of in cuts:
        heights = jax.random.uniform(jax.random.fold_in(jax.random.fold_in(own_key, 6), position), (shards_of,), jnp.float32, smallest / len(cuts), top_value / len(cuts))
        factor_of = factor_of * jnp.repeat(jnp.exp(heights), shape[position] // shards_of).reshape((-1,) + (1,) * (len(shape) - 1 - position))
    return factor_of


def normal_values(key, extent, scale, reach, cuts=(), kind=jnp.bfloat16):
    result = jax.random.normal(key, extent, jnp.float32) * scale
    if len(cuts) > 0:
        result = levels(key, extent, cuts, -0.22, 0.18) * result
    return jnp.clip(result, min=-reach, max=reach).astype(kind)


def setup_inputs(seed: int = 0) -> dict:
    streams_of = jax.random.split(jax.random.key(seed), 16)
    return {
        "h_band": normal_values(streams_of[0], (MICRO, NODES, L), 1.0, 6.0, ((1, 128),)),
        "edges_in": normal_values(streams_of[1], (MICRO, EDGES, L), 1.0, 6.0, ((1, 128),)),
        "band_pick": draw_band_pick(jax.random.fold_in(streams_of[15], 71), 0),
        "senders": draw_senders(jax.random.fold_in(streams_of[15], 71), 0),
        "receivers": draw_receivers(jax.random.fold_in(streams_of[15], 71), 0),
        "halo_rows": draw_halo_rows(jax.random.fold_in(streams_of[15], 71), 0),
        "w_edge_in": normal_values(streams_of[6], (3 * L, L), (3 * L) ** -0.5, 0.21875, ((0, 128),)),
        "w_edge_out": normal_values(streams_of[7], (L, L), L ** -0.5, 0.375, ((0, 128),)),
        "w_node_in": normal_values(streams_of[8], (2 * L, L), (2 * L) ** -0.5, 0.25, ((0, 128),)),
        "w_node_out": normal_values(streams_of[9], (L, L), L ** -0.5, 0.375, ((0, 128),)),
        "biases": normal_values(streams_of[10], (L, 4), 0.5, 3.0, ((0, 128),)),
        "norm_gain": jnp.clip(1.0 + 0.18 * jax.random.normal(streams_of[11], (L, 2), jnp.float32), 0.099609375, 1.8984375).astype(jnp.bfloat16),
        "norm_shift": normal_values(streams_of[12], (L, 2), 0.5, 3.0, ((0, 128),)),
        "cot_nodes": normal_values(streams_of[13], (MICRO, NODES, L), 1.0, 6.0, ((1, 128),)),
        "cot_edges": normal_values(streams_of[14], (MICRO, EDGES, L), 1.0, 6.0, ((1, 128),)),
    }


@jax.custom_vjp
def low(v):
    return lax.optimization_barrier(v.astype(jnp.bfloat16)).astype(jnp.float32)

@jax.custom_vjp
def low_back(v):
    return v

def low_keep(v):
    return (low(v), None)

def low_pass(kept, grad):
    return (grad,)

def back_keep(v):
    return (v, None)

def back_low(kept, grad):
    return (low(grad),)
low.defvjp(low_keep, low_pass)
low_back.defvjp(back_keep, back_low)
epsilon = 1e-05

def matmul(left, right):
    return jnp.dot(left, right, precision=lax.Precision.HIGHEST, preferred_element_type=jnp.float32)

def layer_norm(values, gain, shift):
    center = values - lax.optimization_barrier(jnp.mean(values, axis=-1, keepdims=True))
    spread = lax.rsqrt(lax.optimization_barrier(jnp.mean(center * center, axis=-1, keepdims=True)) + epsilon)
    return center * spread * gain + shift

def to_faces(band, band_pick):
    device_count = N_FACE * N_SUB
    share = NODE_DEV // N_FACE
    picked = jnp.take_along_axis(band.reshape(device_count, NODE_DEV, L), band_pick.reshape(device_count, NODE_DEV, 1), axis=1)
    picked = picked.reshape(N_FACE, N_SUB, N_FACE, share, L)
    return jnp.transpose(picked, (2, 1, 0, 3, 4)).reshape(device_count, NODE_DEV, L)

def to_bands(faces, band_pick):
    device_count = N_FACE * N_SUB
    share = NODE_DEV // N_FACE
    buffer = jnp.transpose(faces.reshape(N_FACE, N_SUB, N_FACE, share, L), (2, 1, 0, 3, 4)).reshape(device_count, NODE_DEV, L)
    placed = jax.vmap(lambda rows, order: jnp.zeros_like(rows).at[order].set(rows))(buffer, band_pick.reshape(device_count, NODE_DEV))
    return placed.reshape(device_count * NODE_DEV, L)

def one_device(params, items):
    w_edge_in, w_edge_out, w_node_in, w_node_out, biases, gains, shifts = params
    h_face, halo_in, edge_rows, sender_ids, receiver_ids = items
    table = jnp.concatenate([h_face, halo_in], axis=0)
    joined = jnp.concatenate([table[sender_ids], h_face[receiver_ids], edge_rows], axis=1)
    first = low_back(matmul(joined, w_edge_in) + biases[:, 0])
    hidden = low(jax.nn.silu(first))
    second = low_back(matmul(hidden, w_edge_out) + biases[:, 1])
    edge_new = low(edge_rows + layer_norm(second, gains[:, 0], shifts[:, 0]))
    summed = low(jax.ops.segment_sum(edge_new, receiver_ids, num_segments=NODE_DEV))
    node_first = low_back(matmul(jnp.concatenate([h_face, summed], axis=1), w_node_in) + biases[:, 2])
    node_hidden = low(jax.nn.silu(node_first))
    node_second = low_back(matmul(node_hidden, w_node_out) + biases[:, 3])
    return (edge_new, h_face + layer_norm(node_second, gains[:, 1], shifts[:, 1]))

def reference(h_band, edges_in, band_pick, senders, receivers, halo_rows, w_edge_in, w_edge_out, w_node_in, w_node_out, biases, norm_gain, norm_shift, cot_nodes, cot_edges):
    device_count = N_FACE * N_SUB
    stepper = jax.checkpoint(one_device)

    def forward(nodes, edges, params):
        node_list = []
        edge_list = []
        for micro_index in range(MICRO):
            h_face = low_back(to_faces(nodes[micro_index], band_pick))
            grouped = h_face.reshape(N_FACE, N_SUB, NODE_DEV, L)
            bound = jnp.take_along_axis(grouped, halo_rows.reshape(N_FACE, N_SUB, HALO, 1), axis=2)
            halo_in = jnp.concatenate([jnp.roll(bound, 1, axis=0), jnp.roll(bound, -1, axis=0)], axis=2)
            halo_in = low_back(halo_in.reshape(device_count, 2 * HALO, L))
            items = (h_face, halo_in, edges[micro_index].reshape(device_count, EDGE_DEV, L), senders.reshape(device_count, EDGE_DEV), receivers.reshape(device_count, EDGE_DEV))
            edge_new, node_new = lax.map(lambda single: stepper(params, single), items)
            node_list.append(to_bands(node_new, band_pick))
            edge_list.append(edge_new.reshape(device_count * EDGE_DEV, L))
        return (jnp.stack(node_list), jnp.stack(edge_list))
    params = tuple((item.astype(jnp.float32) for item in (w_edge_in, w_edge_out, w_node_in, w_node_out, biases, norm_gain, norm_shift)))
    outputs, pullback = jax.vjp(forward, h_band.astype(jnp.float32), edges_in.astype(jnp.float32), params)
    grad_h, grad_e, grad_params = pullback((cot_nodes.astype(jnp.float32), cot_edges.astype(jnp.float32)))
    return (outputs[0].astype(jnp.bfloat16), outputs[1].astype(jnp.bfloat16), grad_h.astype(jnp.bfloat16), grad_e.astype(jnp.bfloat16), grad_params[0], grad_params[1], grad_params[2], grad_params[3], grad_params[4], grad_params[5], grad_params[6])
```

```python
import functools

import jax
import jax.numpy as jnp
from jax import lax
from jax.experimental import pallas as pl
from jax.experimental.pallas import tpu as pltpu
from jax.sharding import PartitionSpec as P

F32, BF = jnp.float32, jnp.bfloat16
EPS = 1e-05
MESH = pl.DeviceIdType.MESH
VMEM = pl.BlockSpec(memory_space=pltpu.VMEM)
ANY = pl.BlockSpec(memory_space=pl.ANY)


def dot(a, b):
    return jnp.dot(a, b, preferred_element_type=F32)


def dot_nt(a, b):
    return lax.dot_general(a, b, (((1,), (1,)), ((), ())), preferred_element_type=F32)


def dot_tn(a, b):
    return lax.dot_general(a, b, (((0,), (0,)), ((), ())), preferred_element_type=F32)


def onehot(col, count):
    lane = lax.broadcasted_iota(jnp.int32, col.shape, 1)
    parts = [(col == lane + 128 * k).astype(F32).astype(BF) for k in range(count // 128)]
    return jnp.concatenate(parts, axis=1)


def onehot_t(row, count):
    spot = lax.broadcasted_iota(jnp.int32, (count, row.shape[1]), 0)
    return (spot == row).astype(F32).astype(BF)


def column(row):
    return jnp.broadcast_to(row, (128, 128)).T


def colsum(values):
    return jnp.sum(values, axis=0, keepdims=True)


def greet(faces, subs):
    me_f, me_s = lax.axis_index("face"), lax.axis_index("sub")
    barrier = pltpu.get_barrier_semaphore()

    def face_signal(k, carry):
        pl.semaphore_signal(
            barrier, inc=1, device_id=(lax.rem(me_f + k, faces), me_s), device_id_type=MESH
        )
        return carry

    def sub_signal(k, carry):
        pl.semaphore_signal(
            barrier, inc=1, device_id=(me_f, lax.rem(me_s + k, subs)), device_id_type=MESH
        )
        return carry

    lax.fori_loop(1, faces, face_signal, 0)
    lax.fori_loop(1, subs, sub_signal, 0)
    pl.semaphore_wait(barrier, faces + subs - 2)


class Spread:
    def __init__(self, axis, count, size, src, dst, send, recv):
        self.axis, self.count, self.size = axis, count, size
        self.src, self.dst, self.send, self.recv = src, dst, send, recv

    def copy(self, k):
        me_f, me_s = lax.axis_index("face"), lax.axis_index("sub")
        me = me_f if self.axis == "face" else me_s
        peer = lax.rem(me + k, self.count)
        device = (peer, me_s) if self.axis == "face" else (me_f, peer)
        rows = pl.ds(pl.multiple_of(me * self.size, self.size), self.size)
        return pltpu.make_async_remote_copy(
            src_ref=self.src(peer),
            dst_ref=self.dst.at[rows],
            send_sem=self.send.at[k],
            recv_sem=self.recv.at[k],
            device_id=device,
            device_id_type=MESH,
        )

    def start(self):
        def go(k, carry):
            self.copy(k).start()
            return carry

        lax.fori_loop(1, self.count, go, 0)

    def wait_recv(self):
        def go(k, carry):
            self.copy(k).wait_recv()
            return carry

        lax.fori_loop(1, self.count, go, 0)

    def wait_send(self):
        def go(k, carry):
            self.copy(k).wait_send()
            return carry

        lax.fori_loop(1, self.count, go, 0)


def block_of(ref, size):
    return lambda peer: ref.at[pl.ds(pl.multiple_of(peer * size, size), size)]


def shift_copies(src, dst, half, faces, sems):
    me_f, me_s = lax.axis_index("face"), lax.axis_index("sub")
    up, down = lax.rem(me_f + 1, faces), lax.rem(me_f + faces - 1, faces)
    return [
        pltpu.make_async_remote_copy(
            src_ref=src[i],
            dst_ref=dst.at[pl.ds(i * half, half)],
            send_sem=sems.at[2 * i],
            recv_sem=sems.at[2 * i + 1],
            device_id=((up, down)[i], me_s),
            device_id_type=MESH,
        )
        for i in range(2)
    ]


def in_kernel(
    faces, subs,
    h_band, cot, pick, halo_rows, wei_s, weo_s, wni_s, wno_s, bias_s, gain_s, shift_s,
    h_face, g_face, halo, wei, weo, wni, wno, small,
    hcat, hpick, gpick, pcol, pack, wz, wall, wide, stage, bound,
    z_send, z_recv, w_send, w_recv, h_send, h_recv, g_send, g_recv, b_sem,
):
    me_f, me_s = lax.axis_index("face"), lax.axis_index("sub")
    nodes, two = h_face.shape
    width = two // 2
    share = nodes // faces
    ra, rb, rc = wei_s.shape[0], weo_s.shape[0], wni_s.shape[0]
    rows = ra + 3 * rb + rc
    devices = faces * subs
    half = halo_rows.shape[1]

    pack[...] = jnp.zeros_like(pack)
    pack[0:ra, :] = wei_s[...].astype(F32)
    pack[ra : ra + rb, :] = weo_s[...].astype(F32)
    pack[ra + rb : ra + rb + rc, :] = wni_s[...].astype(F32)
    pack[ra + rb + rc : ra + 2 * rb + rc, :] = wno_s[...].astype(F32)
    pack[ra + 2 * rb + rc :, 0:4] = bias_s[...].astype(F32)
    pack[ra + 2 * rb + rc :, 4:6] = gain_s[...].astype(F32)
    pack[ra + 2 * rb + rc :, 6:8] = shift_s[...].astype(F32)
    mine = pl.ds(pl.multiple_of(me_s * rows, rows), rows)
    wz[mine, :] = pack[...].astype(BF)
    z_move = Spread("sub", subs, rows, lambda peer: wz.at[mine], wz, z_send, z_recv)
    size_w = subs * rows
    w_move = Spread("face", faces, size_w, lambda peer: wz, wall, w_send, w_recv)
    h_move = Spread("face", faces, share, block_of(hpick, share), h_face, h_send, h_recv)
    g_move = Spread("face", faces, share, block_of(gpick, share), g_face, g_send, g_recv)

    def make_col(j, carry):
        pcol[pl.ds(pl.multiple_of(j * 128, 128), 128), :] = column(pick[pl.ds(j, 1), :])
        return carry

    lax.fori_loop(0, nodes // 128, make_col, 0)
    block = min(256, nodes)

    def select(src, dst):
        for m in range(2):
            hcat[:, m * width : (m + 1) * width] = src[m]

        def go(i, carry):
            at = pl.ds(pl.multiple_of(i * block, block), block)
            dst[at, :] = dot(onehot(pcol[at, :], nodes), hcat[...]).astype(BF)
            return carry

        lax.fori_loop(0, nodes // block, go, 0)

    own = pl.ds(pl.multiple_of(me_f * share, share), share)
    select(h_band, hpick)
    greet(faces, subs)
    z_move.start()
    h_move.start()
    h_face[own, :] = hpick[own, :]
    z_move.wait_recv()
    w_move.start()
    wall[pl.ds(pl.multiple_of(me_f * size_w, size_w), size_w), :] = wz[...]
    select(cot, gpick)
    g_move.start()
    g_face[own, :] = gpick[own, :]
    h_move.wait_recv()
    hcol = column(halo_rows[...])
    bound[...] = dot(onehot(hcol, nodes), h_face[...]).astype(BF)
    b_move = shift_copies((bound, bound), halo, half, faces, b_sem)
    for one in b_move:
        one.start()
    w_move.wait_recv()
    for c in range(width // 128):
        wide[c] = wall[:, c * 128 : (c + 1) * 128].astype(F32)
    low, high = 0, ra
    for out, count in ((wei, ra), (weo, rb), (wni, rc), (wno, rb)):
        for i in range(count):
            for c in range(width // 128):
                stage[c, pl.ds(i, devices, stride=count), :] = wide[
                    c, pl.ds(low + i, devices, stride=rows), :
                ]
        for c in range(width // 128):
            out[:, c * 128 : (c + 1) * 128] = stage[c, 0 : devices * count, :].astype(BF)
        low += count
    total = jnp.zeros((128, width), F32)
    for i in range(rb):
        part = wide[0, pl.ds(low + i, devices, stride=rows), :].astype(BF)
        spot = lax.broadcasted_iota(jnp.int32, (devices, width), 1)
        source = lax.broadcasted_iota(jnp.int32, (devices, width), 0)
        total += dot_tn(part, (spot == source * rb + i).astype(F32).astype(BF))
    small[...] = total[0:8, :]
    g_move.wait_recv()
    for one in b_move:
        one.wait_recv()
        one.wait_send()
    for move in (z_move, h_move, w_move, g_move):
        move.wait_send()


def gather_in(faces, subs, h_band, cot, pick, halo_rows, shards):
    nodes, width = h_band.shape[1:]
    half = halo_rows.shape[1]
    counts = [s.shape[0] for s in shards[:4]]
    rows = sum(counts) + counts[1]
    devices = faces * subs
    S = jax.ShapeDtypeStruct
    two = 2 * width
    sem = pltpu.SemaphoreType.DMA
    return pl.pallas_call(
        functools.partial(in_kernel, faces, subs),
        out_shape=(
            S((nodes, two), BF), S((nodes, two), BF), S((2 * half, two), BF),
            *[S((c * devices, width), BF) for c in counts], S((8, width), F32),
        ),
        in_specs=[VMEM] * 11,
        out_specs=tuple([VMEM] * 8),
        scratch_shapes=[
            pltpu.VMEM((nodes, two), BF), pltpu.VMEM((nodes, two), BF), pltpu.VMEM((nodes, two), BF),
            pltpu.VMEM((nodes, 128), jnp.int32),
            pltpu.VMEM((rows, width), F32), pltpu.VMEM((subs * rows, width), BF),
            pltpu.VMEM((devices * rows, width), BF), pltpu.VMEM((width // 128, devices * rows, 128), F32),
            pltpu.VMEM((width // 128, max(counts) * devices, 128), F32), pltpu.VMEM((half, two), BF),
            sem((subs,)), sem((subs,)), sem((faces,)), sem((faces,)),
            sem((faces,)), sem((faces,)), sem((faces,)), sem((faces,)), sem((4,)),
        ],
        compiler_params=pltpu.CompilerParams(
            collective_id=0, has_side_effects=True, vmem_limit_bytes=40 * 1024 * 1024
        ),
        name="gather_in",
    )(h_band, cot, pick, halo_rows, *shards)


def compute_kernel(
    tile,
    h, halo, g, wei, weo, wni, wno, small, send, recv, edges, cot,
    eo_out, ge_out, nf_out, df_out, dhalo_out, gwei, gweo, gwni, gwno, gsmall,
    e_v, c_v, o_v, slope_v, hid_v, y_v, q_v, scol, rcol, pq, summed, ss, sr, dsum, sems,
):
    count, width = edges.shape[1:]
    nodes = h.shape[0]
    table = nodes + halo.shape[0]
    for m in range(2):
        pltpu.make_async_copy(edges.at[m], e_v.at[m], sems.at[m]).start()
        pltpu.make_async_copy(cot.at[m], c_v.at[m], sems.at[2 + m]).start()

    def make_col(j, carry):
        for src, dst in ((send, scol), (recv, rcol)):
            dst[pl.ds(pl.multiple_of(j * 128, 128), 128), :] = column(src[pl.ds(j, 1), :])
        return carry

    lax.fori_loop(0, count // 128, make_col, 0)
    for ref in (gwei, gweo, gwni, gwno, gsmall):
        ref[...] = jnp.zeros_like(ref)
    b0, b1, b2, b3, gn0, gn1, sh0, sh1 = (small[k : k + 1, :] for k in range(8))
    per = tile // 128

    def index_row(ref, i):
        return jnp.concatenate([ref[pl.ds(i * per + k, 1), :] for k in range(per)], axis=1)

    for m in range(2):
        lanes = slice(m * width, (m + 1) * width)
        hm = h[:, lanes]
        pq[0:nodes, :] = dot(hm, wei[0:width, :]).astype(BF)
        pq[nodes:table, :] = dot(halo[:, lanes], wei[0:width, :]).astype(BF)
        pq[table:, :] = dot(hm, wei[width : 2 * width, :]).astype(BF)
        summed[...] = jnp.zeros_like(summed)
        pltpu.make_async_copy(edges.at[m], e_v.at[m], sems.at[m]).wait()

        def forward(i, carry):
            rows = pl.ds(pl.multiple_of(i * tile, tile), tile)
            e = e_v[m, rows, :]
            first = dot(e, wei[2 * width :, :]) + b0
            first += dot(onehot(scol[rows, :], table), pq[0:table, :])
            first += dot(onehot(rcol[rows, :], nodes), pq[table:, :])
            s = jax.nn.sigmoid(first)
            slope_v[rows, :] = (s * (1.0 + first * (1.0 - s))).astype(BF)
            hidden = (first * s).astype(BF)
            hid_v[rows, :] = hidden
            second = dot(hidden, weo[...]) + b1
            center = second - jnp.mean(second, axis=1, keepdims=True)
            q = lax.rsqrt(jnp.mean(center * center, axis=1, keepdims=True) + EPS)
            y = center * q
            y_v[rows, :] = y.astype(BF)
            q_v[rows, :] = jnp.broadcast_to(q, (tile, 128))
            eo = (e.astype(F32) + (y * gn0 + sh0)).astype(BF)
            o_v[m, rows, :] = eo
            summed[...] += dot(onehot_t(index_row(recv, i), nodes), eo)
            return carry

        lax.fori_loop(0, count // tile, forward, 0)
        pltpu.make_async_copy(o_v.at[m], eo_out.at[m], sems.at[4 + m]).start()
        sm = summed[...].astype(BF)
        nfirst = dot(hm, wni[0:width, :]) + dot(sm, wni[width:, :]) + b2
        sigma = jax.nn.sigmoid(nfirst)
        nhid = (nfirst * sigma).astype(BF)
        second = dot(nhid, wno[...]) + b3
        center = second - jnp.mean(second, axis=1, keepdims=True)
        q = lax.rsqrt(jnp.mean(center * center, axis=1, keepdims=True) + EPS)
        y = center * q
        nf_out[:, lanes] = (hm.astype(F32) + (y * gn1 + sh1)).astype(BF)
        gf = g[:, lanes].astype(F32)
        scaled = gf * gn1
        m1 = jnp.mean(scaled, axis=1, keepdims=True)
        m2 = jnp.mean(scaled * y, axis=1, keepdims=True)
        dn2 = (q * (scaled - m1 - y * m2)).astype(BF)
        slope = sigma * (1.0 + nfirst * (1.0 - sigma))
        dn1 = (dot_nt(dn2, wno[...]) * slope).astype(BF)
        gwno[...] += dot_tn(nhid, dn2)
        gwni[0:width, :] += dot_tn(hm, dn1)
        gwni[width:, :] += dot_tn(sm, dn1)
        gsmall[2:3, :] += colsum(dn1.astype(F32))
        gsmall[3:4, :] += colsum(dn2.astype(F32))
        gsmall[5:6, :] += colsum(gf * y)
        gsmall[7:8, :] += colsum(gf)
        df_out[:, lanes] = gf + dot_nt(dn1, wni[0:width, :])
        dsum[...] = dot_nt(dn1, wni[width:, :]).astype(BF)
        ss[...] = jnp.zeros_like(ss)
        sr[...] = jnp.zeros_like(sr)
        pltpu.make_async_copy(cot.at[m], c_v.at[m], sems.at[2 + m]).wait()

        def backward(i, carry):
            db2, dgain, dshift = carry
            rows = pl.ds(pl.multiple_of(i * tile, tile), tile)
            de = c_v[m, rows, :].astype(F32) + dot(onehot(rcol[rows, :], nodes), dsum[...])
            y = y_v[rows, :].astype(F32)
            scaled = de * gn0
            m1 = jnp.mean(scaled, axis=1, keepdims=True)
            m2 = jnp.mean(scaled * y, axis=1, keepdims=True)
            de2 = (q_v[rows, 0:1] * (scaled - m1 - y * m2)).astype(BF)
            dgain = dgain + colsum(de * y)
            dshift = dshift + colsum(de)
            db2 = db2 + colsum(de2.astype(F32))
            gweo[...] += dot_tn(hid_v[rows, :], de2)
            de1 = (dot_nt(de2, weo[...]) * slope_v[rows, :].astype(F32)).astype(BF)
            gwei[2 * width :, :] += dot_tn(e_v[m, rows, :], de1)
            c_v[m, rows, :] = (de + dot_nt(de1, wei[2 * width :, :])).astype(BF)
            ss[...] += dot(onehot_t(index_row(send, i), table), de1)
            sr[...] += dot(onehot_t(index_row(recv, i), nodes), de1)
            return db2, dgain, dshift

        zero = jnp.zeros((1, width), F32)
        db2, dgain, dshift = lax.fori_loop(0, count // tile, backward, (zero, zero, zero))
        pltpu.make_async_copy(c_v.at[m], ge_out.at[m], sems.at[6 + m]).start()
        gsmall[1:2, :] += db2
        gsmall[4:5, :] += dgain
        gsmall[6:7, :] += dshift
        gsmall[0:1, :] += colsum(sr[...])
        sb = ss[...].astype(BF)
        rb = sr[...].astype(BF)
        gwei[0:width, :] += dot_tn(hm, sb[0:nodes]) + dot_tn(halo[:, lanes], sb[nodes:])
        gwei[width : 2 * width, :] += dot_tn(hm, rb)
        df_out[:, lanes] += dot_nt(sb[0:nodes], wei[0:width, :]) + dot_nt(rb, wei[width : 2 * width, :])
        dhalo_out[:, lanes] = dot_nt(sb[nodes:], wei[0:width, :]).astype(BF)
    for m in range(2):
        pltpu.make_async_copy(o_v.at[m], eo_out.at[m], sems.at[4 + m]).wait()
        pltpu.make_async_copy(c_v.at[m], ge_out.at[m], sems.at[6 + m]).wait()


def compute(h, halo, g, params, send, recv, edges, cot):
    nodes = h.shape[0]
    count, width = edges.shape[1:]
    table = nodes + halo.shape[0]
    tile = min(1024, count)
    S = jax.ShapeDtypeStruct
    V = pltpu.VMEM
    return pl.pallas_call(
        functools.partial(compute_kernel, tile),
        out_shape=(
            S((2, count, width), BF), S((2, count, width), BF), S((nodes, 2 * width), BF),
            S((nodes, 2 * width), F32), S((halo.shape[0], 2 * width), BF),
            S((3 * width, width), F32), S((width, width), F32), S((2 * width, width), F32),
            S((width, width), F32), S((8, width), F32),
        ),
        in_specs=[VMEM] * 10 + [ANY] * 2,
        out_specs=tuple([ANY] * 2 + [VMEM] * 8),
        scratch_shapes=[
            V((2, count, width), BF), V((2, count, width), BF), V((2, count, width), BF),
            V((count, width), BF), V((count, width), BF), V((count, width), BF), V((count, 128), F32),
            V((count, 128), jnp.int32), V((count, 128), jnp.int32),
            V((table + nodes, width), BF), V((nodes, width), F32), V((table, width), F32),
            V((nodes, width), F32), V((nodes, width), BF), pltpu.SemaphoreType.DMA((8,)),
        ],
        compiler_params=pltpu.CompilerParams(vmem_limit_bytes=62 * 1024 * 1024),
        name="compute",
    )(h, halo, g, *params, send, recv, edges, cot)


def out_kernel(
    faces, subs, counts,
    nf, df, dhalo, halo_rows, gwei, gweo, gwni, gwno, gsmall,
    nf_got, df_got, parts,
    dsend, back, stage, pack, zsrc, zgot, fsum, tall, flat,
    b_sem, n_send, n_recv, d_send, d_recv, z_send, z_recv, f_send, f_recv,
):
    me_f, me_s = lax.axis_index("face"), lax.axis_index("sub")
    nodes, two = nf.shape
    width = two // 2
    share = nodes // faces
    half = halo_rows.shape[1]
    rows = sum(counts) + counts[1]
    size_z = faces * rows
    own = pl.ds(pl.multiple_of(me_f * share, share), share)

    greet(faces, subs)
    b_move = shift_copies(
        (dhalo.at[pl.ds(half, half)], dhalo.at[pl.ds(0, half)]), back, half, faces, b_sem
    )
    for one in b_move:
        one.start()
    n_move = Spread("face", faces, share, block_of(nf, share), nf_got, n_send, n_recv)
    n_move.start()
    nf_got[own, :] = nf[own, :]
    tall[...] = jnp.zeros_like(tall)
    tall[0:8, :] = gsmall[...]
    flat[...] = tall[...].T
    pack[...] = jnp.zeros_like(pack)
    low = 0
    for ref, count in zip((gwei, gweo, gwni, gwno), counts):
        for c in range(width // 128):
            lanes = slice(c * 128, (c + 1) * 128)
            stage[0 : ref.shape[0], :] = ref[:, lanes]
            for s in range(subs):
                for i in range(count):
                    pack[c, pl.ds(s * size_z + low + i, faces, stride=rows), :] = stage[
                        pl.ds(s * count + i, faces, stride=subs * count), :
                    ]
        low += count
    for s in range(subs):
        for i in range(counts[1]):
            pack[0, pl.ds(s * size_z + low + i, faces, stride=rows), :] = flat[
                pl.ds(s * counts[1] + i, faces, stride=subs * counts[1]), :
            ]
    for c in range(width // 128):
        zsrc[:, c * 128 : (c + 1) * 128] = pack[c].astype(BF)
    z_move = Spread("sub", subs, size_z, block_of(zsrc, size_z), zgot, z_send, z_recv)
    z_move.start()
    mine = pl.ds(pl.multiple_of(me_s * size_z, size_z), size_z)
    zgot[mine, :] = zsrc[mine, :]
    spread = lax.broadcasted_iota(jnp.int32, (nodes, half), 0)
    place = (spread == halo_rows[...]).astype(F32).astype(BF)
    for one in b_move:
        one.wait_recv()
    for m in range(2):
        lanes = slice(m * width, (m + 1) * width)
        owned = dot(place, back[0:half, lanes]) + dot(place, back[half : 2 * half, lanes])
        dsend[:, lanes] = (df[:, lanes] + owned).astype(BF)
    d_move = Spread("face", faces, share, block_of(dsend, share), df_got, d_send, d_recv)
    d_move.start()
    df_got[own, :] = dsend[own, :]
    z_move.wait_recv()
    total = zgot[0:size_z, :].astype(F32)
    for s in range(1, subs):
        total += zgot[s * size_z : (s + 1) * size_z, :].astype(F32)
    fsum[...] = total
    f_move = Spread("face", faces, rows, block_of(fsum, rows), parts, f_send, f_recv)
    f_move.start()
    slot = pl.ds(pl.multiple_of(me_f * rows, rows), rows)
    parts[slot, :] = fsum[slot, :]
    for move in (n_move, d_move, f_move):
        move.wait_recv()
    for one in b_move:
        one.wait_send()
    for move in (n_move, z_move, d_move, f_move):
        move.wait_send()


def send_out(faces, subs, counts, nf, df, dhalo, halo_rows, grads):
    nodes, two = nf.shape
    width = two // 2
    half = halo_rows.shape[1]
    rows = sum(counts) + counts[1]
    S, V = jax.ShapeDtypeStruct, pltpu.VMEM
    sem = pltpu.SemaphoreType.DMA
    size_z = faces * rows
    return pl.pallas_call(
        functools.partial(out_kernel, faces, subs, counts),
        out_shape=(S((nodes, two), BF), S((nodes, two), BF), S((size_z, width), F32)),
        in_specs=[VMEM] * 9,
        out_specs=(VMEM, VMEM, VMEM),
        scratch_shapes=[
            V((nodes, two), BF), V((2 * half, two), BF), V((counts[0] * faces * subs, 128), F32),
            V((width // 128, subs * size_z, 128), F32), V((subs * size_z, width), BF), V((subs * size_z, width), BF), V((size_z, width), F32),
            V((128, width), F32), V((width, 128), F32),
            sem((4,)), sem((faces,)), sem((faces,)), sem((faces,)), sem((faces,)),
            sem((subs,)), sem((subs,)), sem((faces,)), sem((faces,)),
        ],
        compiler_params=pltpu.CompilerParams(
            collective_id=1, has_side_effects=True, vmem_limit_bytes=40 * 1024 * 1024
        ),
        name="send_out",
    )(nf, df, dhalo, halo_rows, *grads)


def final_kernel(
    faces, counts, nf_got, df_got, parts, pick,
    node_out, grad_nodes, o0, o1, o2, o3, o4, o5, o6,
):
    nodes, two = nf_got.shape
    width = two // 2
    index = jnp.concatenate([pick[k : k + 1, :] for k in range(nodes // 128)], axis=1)
    block = min(256, nodes)
    for b in range(nodes // block):
        spot = lax.broadcasted_iota(jnp.int32, (block, nodes), 0) + b * block
        place = (spot == index).astype(F32).astype(BF)
        rows = pl.ds(b * block, block)
        for src, out in ((nf_got, node_out), (df_got, grad_nodes)):
            moved = dot(place, src[...]).astype(BF)
            for m in range(2):
                out[m, rows, :] = moved[:, m * width : (m + 1) * width]
    rows = sum(counts) + counts[1]
    total = parts[0:rows, :]
    for p in range(1, faces):
        total += parts[p * rows : (p + 1) * rows, :]
    at = 0
    for out, count in zip((o0, o1, o2, o3), counts):
        out[...] = total[at : at + count, :]
        at += count
    o4[...] = total[at:, 0:4]
    o5[...] = total[at:, 4:6]
    o6[...] = total[at:, 6:8]


def finish(faces, counts, nf_got, df_got, parts, pick):
    nodes, two = nf_got.shape
    width = two // 2
    S = jax.ShapeDtypeStruct
    return pl.pallas_call(
        functools.partial(final_kernel, faces, counts),
        out_shape=(
            S((2, nodes, width), BF), S((2, nodes, width), BF),
            *[S((c, width), F32) for c in counts],
            S((counts[1], 4), F32), S((counts[1], 2), F32), S((counts[1], 2), F32),
        ),
        in_specs=[VMEM] * 4,
        out_specs=tuple([VMEM] * 9),
        compiler_params=pltpu.CompilerParams(vmem_limit_bytes=40 * 1024 * 1024),
        name="finish",
    )(nf_got, df_got, parts, pick)


def body(
    faces, subs,
    h_band, edges_in, band_pick, senders, receivers, halo_rows,
    w_edge_in, w_edge_out, w_node_in, w_node_out, biases, norm_gain, norm_shift,
    cot_nodes, cot_edges,
):
    pick = band_pick.reshape(-1, 128)
    offered = halo_rows.reshape(1, -1)
    send = senders.reshape(-1, 128)
    recv = receivers.reshape(-1, 128)
    shards = (w_edge_in, w_edge_out, w_node_in, w_node_out, biases, norm_gain, norm_shift)
    counts = tuple(s.shape[0] for s in shards[:4])
    h, g, halo, *params = gather_in(faces, subs, h_band, cot_nodes, pick, offered, shards)
    edge_out, grad_edges, nf, df, dhalo, *grads = compute(
        h, halo, g, params, send, recv, edges_in, cot_edges
    )
    nf_got, df_got, parts = send_out(faces, subs, counts, nf, df, dhalo, offered, grads)
    node_out, grad_nodes, *weights = finish(faces, counts, nf_got, df_got, parts, pick)
    return (node_out, edge_out, grad_nodes, grad_edges, *weights)


def solution(mesh):
    both = ("face", "sub")
    rows, items = P(both, None), P(None, both, None)
    in_specs = (items, items, P(both), P(both), P(both), P(both)) + (rows,) * 7 + (items, items)
    out_specs = (items,) * 4 + (rows,) * 7
    return jax.shard_map(
        functools.partial(body, mesh.shape["face"], mesh.shape["sub"]),
        mesh=mesh, in_specs=in_specs, out_specs=out_specs, check_vma=False,
    )
```
